32 devices in a mesh: dom: 2 (over core), gx: 4 (over y, x), gy: 4 (over z).
Axes of the slice: x: 2, y: 2, z: 4, core: 2. Of those that a mesh axis runs over, the one named last changes fastest.
Arguments:
- velocity: float32 [2, 3, 64, 32, 128], P('dom', None, 'gx', 'gy'), may hold values from -5 to 5
- fringe_start: int32 [1], replicated, may hold values from 0 to 63
Outputs:
- velocity_out: float32 [2, 3, 64, 32, 128], P('dom', None, 'gx', 'gy')
- spectrum: float32 [2, 128, 64, 32], P(None, ('dom', 'gx'), 'gy')
The draws below stay inside these ranges and needn't reach their ends.
All inputs are finite; a program needn't handle non-finite values.
Results may differ from the reference program's by a relative error of at most 0.000084.
Values sent between devices are 32-bit elements; how exact they have to be, the bound alone decides.
A program may use at most 64 MiB of HBM per device.

```python
import math
import jax
import jax.numpy as jnp

NZ = 128
NX = 64
NY = 32
FRINGE = 32


def steps_of(stream_key, dims, cuts, low, top_value):
    gain, own = 1.0, jax.random.fold_in(stream_key, 6)
    for dim, blocks in cuts:
        draws = jnp.exp(jax.random.uniform(jax.random.fold_in(own, dim), (blocks,), jnp.float32, low / len(cuts), top_value / len(cuts)))
        gain = gain * jnp.repeat(draws, dims[dim] // blocks).reshape([-1 if axis == dim else 1 for axis in range(len(dims))])
    return gain


def normal_values(key, dims, deviation, most, pieces=(), held_as=jnp.bfloat16):
    factor_of = steps_of(key, dims, pieces, -0.22, 0.18) if pieces else 1.0
    result = jax.random.normal(key, dims, jnp.float32) * deviation * factor_of
    return jnp.minimum(jnp.maximum(result, -most), most).astype(held_as)


def setup_inputs(seed: int = 0) -> dict:
    arg_keys = jax.random.split(jax.random.key(seed), 3)
    return {
        "velocity": normal_values(arg_keys[0], (2, 3, NX, NY, NZ), 1.0, 5.0, ((0, 2), (2, 4), (3, 4)), jnp.float32),
        "fringe_start": jax.random.randint(arg_keys[1], (1,), 0, NX).astype(jnp.int32),
    }


time_step = 0.1
fringe_rate = 1.0
smag_coef = 0.03
base_visc = 0.02
strain_floor = 0.25

def combine(center, x_plus, x_minus, y_plus, y_minus, z_plus, z_minus, inflow, fringe_ramp):
    grad_x = 0.5 * (x_plus - x_minus)
    grad_y = 0.5 * (y_plus - y_minus)
    grad_z = 0.5 * (z_plus - z_minus)
    gradients = (grad_x, grad_y, grad_z)
    strain = jnp.zeros_like(center[0])
    for comp_a in range(3):
        for comp_b in range(3):
            sym_part = 0.5 * (gradients[comp_b][comp_a] + gradients[comp_a][comp_b])
            strain = strain + sym_part * sym_part
    eddy_visc = base_visc + smag_coef * jnp.sqrt(2.0 * strain + strain_floor)
    advection = center[0] * grad_x + center[1] * grad_y + center[2] * grad_z
    laplace_term = x_plus + x_minus + y_plus + y_minus + z_plus + z_minus - 6.0 * center
    return -advection + eddy_visc * laplace_term + fringe_ramp * (inflow - center)

def ramp_values(fringe_start, x_cells, fringe_len, total_len):
    offset = (x_cells - fringe_start[0] + total_len) % total_len
    inside = offset < fringe_len
    sine_part = jnp.sin((offset.astype(jnp.float32) + 0.5) * (math.pi / fringe_len))
    return jnp.where(inside, fringe_rate * sine_part * sine_part, 0.0)

def periodic_tendency(field, inflow, fringe_ramp):
    padded = jnp.pad(field, ((0, 0), (0, 0), (0, 0), (1, 1)))
    return combine(field, jnp.roll(field, -1, 1), jnp.roll(field, 1, 1), jnp.roll(field, -1, 2), jnp.roll(field, 1, 2), padded[..., 2:], padded[..., :-2], inflow, fringe_ramp)

def reference(velocity, fringe_start):
    x_cells = jnp.arange(NX, dtype=jnp.int32)
    fringe_ramp = ramp_values(fringe_start, x_cells, FRINGE, NX).reshape(NX, 1, 1)
    inflow = velocity[0]
    results = []
    for domain in range(2):
        start_field = velocity[domain]
        ramp_here = fringe_ramp * float(domain)
        section_one = start_field + time_step * periodic_tendency(start_field, inflow, ramp_here)
        section_two = 0.75 * start_field + 0.25 * (section_one + time_step * periodic_tendency(section_one, inflow, ramp_here))
        section_three = 1.0 / 3.0 * start_field + 2.0 / 3.0 * (section_two + time_step * periodic_tendency(section_two, inflow, ramp_here))
        results.append(section_three)
    farm_field = results[1]
    padded = jnp.pad(farm_field[2], ((0, 0), (0, 0), (1, 1)))
    divergence = 0.5 * (jnp.roll(farm_field[0], -1, 0) - jnp.roll(farm_field[0], 1, 0)) + 0.5 * (jnp.roll(farm_field[1], -1, 1) - jnp.roll(farm_field[1], 1, 1)) + 0.5 * (padded[:, :, 2:] - padded[:, :, :-2])
    transform = jnp.fft.fft2(divergence, axes=(0, 1), norm='ortho')
    transform = jnp.transpose(transform, (2, 0, 1))
    spectrum = jnp.stack([jnp.real(transform), jnp.imag(transform)]).astype(jnp.float32)
    return (jnp.stack(results), spectrum)
```

```python
import functools
import math

import jax
import jax.numpy as jnp
import numpy as np
from jax import lax
from jax.experimental import pallas as pl
from jax.experimental.pallas import tpu as pltpu
from jax.sharding import PartitionSpec as P

time_step = 0.1
fringe_rate = 1.0
smag_coef = 0.03
base_visc = 0.02
strain_floor = 0.25
MESH = pl.DeviceIdType.MESH
WIDE = 4
BASE = 8


def from_behind(shard, axis, by):
    peers = lax.axis_size(axis)
    pairs = [(i, i + by) for i in range(peers) if 0 <= i + by < peers]
    return lax.ppermute(shard, axis, pairs)


def partner_half(values):
    return from_behind(values, "dom", -1)


def dft_tables(length):
    positions = jnp.arange(length, dtype=jnp.int32)
    phase = (positions[:, None] * positions[None, :] % length).astype(jnp.float32) * (
        2.0 * math.pi / length
    )
    factor = 1.0 / math.sqrt(length)
    return (jnp.cos(phase) * factor, jnp.sin(phase) * factor)


def step_kernel(sizes, fused, *refs):
    tiles_x, tiles_y, cells_x, cells_y, levels_z, fringe_len = sizes
    if fused:
        (fs_ref, u_hbm, tx_hbm, ty_hbm, v_hbm, spec_ref, *scratch) = refs
    else:
        (fs_ref, u_hbm, v_hbm, div_ref, *scratch) = refs
    (U, I, S1, S2, S3, edge, near, near_in, diag, diag_in, ramp) = scratch[:11]
    (load_sem, send_sem, recv_sem, in_send, in_recv, out_sem) = scratch[11:17]
    if fused:
        tx, ty, rows, block, got, turned, tab_sem, blk_send, blk_recv, own_sem = scratch[17:]
    dom, gx, gy = (lax.axis_index(name) for name in ("dom", "gx", "gy"))
    count = 2 * tiles_x * tiles_y
    me = (dom * tiles_x + gx) * tiles_y + gy
    total_x = cells_x * tiles_x
    hi = WIDE + cells_x
    inner = pl.ds(BASE, cells_y)

    def at(index):
        return (
            index // (tiles_x * tiles_y),
            lax.rem(index // tiles_y, tiles_x),
            lax.rem(index, tiles_y),
        )

    def beside(domain, dx, dy):
        return (
            domain,
            lax.rem(gx + dx + tiles_x, tiles_x),
            lax.rem(gy + dy + tiles_y, tiles_y),
        )

    around = [(1, 0), (-1, 0), (0, 1), (0, -1), (1, 1), (1, -1), (-1, 1), (-1, -1)]
    barrier = pltpu.get_barrier_semaphore()
    if fused:
        @pl.loop(1, count)
        def _(i):
            pl.semaphore_signal(
                barrier, inc=1, device_id=at(lax.rem(me + i, count)), device_id_type=MESH
            )
    else:
        for dx, dy in around:
            for domain in range(2):
                pl.semaphore_signal(
                    barrier, inc=1, device_id=beside(domain, dx, dy), device_id_type=MESH
                )
        pl.semaphore_signal(barrier, inc=1, device_id=beside(1 - dom, 0, 0), device_id_type=MESH)

    load = pltpu.make_async_copy(u_hbm.at[0], U.at[:, pl.ds(WIDE, cells_x), inner, :], load_sem)
    load.start()
    if fused:
        tab_x = pltpu.make_async_copy(tx_hbm.at[gy], tx, tab_sem.at[0])
        tab_y = pltpu.make_async_copy(ty_hbm, ty, tab_sem.at[1])
        tab_x.start()
        tab_y.start()

    cell = lax.broadcasted_iota(jnp.int32, ramp.shape, 0) + (gx * cells_x - WIDE)
    offset = cell - fs_ref[0]
    for _ in range(2):
        offset = jnp.where(offset < 0, offset + total_x, offset)
    offset = jnp.where(offset >= total_x, offset - total_x, offset)
    sine = jnp.sin((offset.astype(jnp.float32) + 0.5) * (math.pi / fringe_len))
    farm = dom.astype(jnp.float32)
    ramp[...] = jnp.where(offset < fringe_len, fringe_rate * sine * sine, 0.0) * farm

    @pl.when(dom == 0)
    def _():
        I[...] = jnp.zeros_like(I)

    load.wait()
    edge[0] = U[:, WIDE:hi, BASE : BASE + WIDE, :]
    edge[1] = U[:, WIDE:hi, BASE + cells_y - WIDE : BASE + cells_y, :]
    pl.semaphore_wait(barrier, count - 1 if fused else 17)

    def margins(domain, field, strips, corners, sends, recvs):
        low, high = pl.ds(0, WIDE), pl.ds(hi, WIDE)
        pieces = []
        for dx, dy in around:
            mine = pl.ds(cells_x, WIDE) if dx > 0 else pl.ds(WIDE, WIDE)
            if dy == 0:
                pieces.append((U.at[:, mine, inner, :], field.at[:, low if dx > 0 else high, inner, :]))
            elif dx == 0:
                pieces.append((edge.at[1 if dy > 0 else 0], strips.at[0 if dy > 0 else 1]))
            else:
                part = pl.ds(cells_x - WIDE if dx > 0 else 0, WIDE)
                pieces.append((
                    edge.at[1 if dy > 0 else 0, :, part],
                    corners.at[0 if dx > 0 else 1, 0 if dy > 0 else 1],
                ))
        return [
            pltpu.make_async_remote_copy(
                src_ref=source, dst_ref=target, send_sem=sends.at[i], recv_sem=recvs.at[i],
                device_id=beside(domain, *around[i]), device_id_type=MESH,
            )
            for i, (source, target) in enumerate(pieces)
        ]

    def place(field, strips, corners):
        for side in range(2):
            span = pl.ds(BASE - WIDE if side == 0 else BASE + cells_y, WIDE)
            field[:, WIDE:hi, span, :] = strips[side]
            field[:, 0:WIDE, span, :] = corners[0, side]
            field[:, hi : hi + WIDE, span, :] = corners[1, side]

    own = margins(dom, U, near, diag, send_sem, recv_sem)
    inflow = margins(1, I, near_in, diag_in, in_send, in_recv)
    block_in = pltpu.make_async_remote_copy(
        src_ref=U.at[:, pl.ds(WIDE, cells_x), inner, :],
        dst_ref=I.at[:, pl.ds(WIDE, cells_x), inner, :],
        send_sem=in_send.at[8], recv_sem=in_recv.at[8],
        device_id=(1 - dom, gx, gy), device_id_type=MESH,
    )
    order = [4, 5, 6, 7, 2, 3, 0, 1]
    for i in order:
        own[i].start()

    @pl.when(dom == 0)
    def _():
        for i in order:
            inflow[i].start()
        block_in.start()

    for copy in own:
        copy.wait_recv()
    place(U, near, diag)

    @pl.when(dom == 1)
    def _():
        for copy in inflow:
            copy.wait_recv()
        block_in.wait_recv()
        place(I, near_in, diag_in)

    lane = lax.broadcasted_iota(jnp.int32, (8, levels_z), 1)
    first, last = lane == 0, lane == levels_z - 1

    def rate(field, x, row):
        centre = [field[c, x, pl.ds(row, 8), :] for c in range(3)]
        grads, laps = [[], [], []], []
        for c in range(3):
            xp, xm = field[c, x + 1, pl.ds(row, 8), :], field[c, x - 1, pl.ds(row, 8), :]
            yp, ym = field[c, x, pl.ds(row + 1, 8), :], field[c, x, pl.ds(row - 1, 8), :]
            zp = jnp.where(last, 0.0, pltpu.roll(centre[c], levels_z - 1, 1))
            zm = jnp.where(first, 0.0, pltpu.roll(centre[c], 1, 1))
            grads[0].append(xp - xm)
            grads[1].append(yp - ym)
            grads[2].append(zp - zm)
            laps.append((xp + xm) + (yp + ym) + (zp + zm) - 6.0 * centre[c])
        (axx, axy, axz), (ayx, ayy, ayz), (azx, azy, azz) = grads
        shear = (axy + ayx, axz + azx, ayz + azy)
        diagonal = axx * axx + ayy * ayy + azz * azz
        sheared = shear[0] * shear[0] + shear[1] * shear[1] + shear[2] * shear[2]
        under = 0.5 * diagonal + (0.25 * sheared + strain_floor)
        eddy = base_visc + smag_coef * (under * lax.rsqrt(under))
        pull = jnp.broadcast_to(ramp[pl.ds(x, 1), :], (8, levels_z))
        rates = []
        for c in range(3):
            carried = centre[0] * grads[0][c] + centre[1] * grads[1][c] + centre[2] * grads[2][c]
            behind = I[c, x, pl.ds(row, 8), :] - centre[c]
            rates.append(eddy * laps[c] - 0.5 * carried + pull * behind)
        return centre, rates

    def stage(field, result, margin, finish):
        starts = (BASE - margin, BASE + cells_y + margin - 8)

        @pl.loop(WIDE - margin, hi + margin)
        def _(x):
            for row in starts:
                centre, rates = rate(field, x, row)
                for c in range(3):
                    result[c, x, pl.ds(row, 8), :] = finish(
                        U[c, x, pl.ds(row, 8), :], centre[c] + time_step * rates[c]
                    )

    stage(U, S1, 3, lambda start, moved: moved)
    stage(S1, S2, 2, lambda start, moved: 0.75 * start + 0.25 * moved)
    stage(S2, S3, 1, lambda start, moved: (1.0 / 3.0) * start + (2.0 / 3.0) * moved)

    out = pltpu.make_async_copy(S3.at[:, pl.ds(WIDE, cells_x), inner, :], v_hbm.at[0], out_sem)
    out.start()

    def divergence(x):
        w = S3[2, x, inner, :]
        up = jnp.where(last, 0.0, pltpu.roll(w, levels_z - 1, 1))
        down = jnp.where(first, 0.0, pltpu.roll(w, 1, 1))
        along = 0.5 * (S3[0, x + 1, inner, :] - S3[0, x - 1, inner, :])
        across = 0.5 * (S3[1, x, pl.ds(BASE + 1, 8), :] - S3[1, x, pl.ds(BASE - 1, 8), :])
        return along + across + 0.5 * (up - down)

    if not fused:
        for x in range(cells_x):
            div_ref[x] = divergence(x + WIDE)
    else:
        parts = 2 * tiles_x
        depth = levels_z // parts
        group = lax.broadcasted_iota(jnp.int32, (cells_x, levels_z), 1) // depth

        def block_copy(i):
            target = lax.rem(me + i, count)
            return pltpu.make_async_remote_copy(
                src_ref=block.at[target // tiles_y], dst_ref=got.at[gy, gx],
                send_sem=blk_send.at[i], recv_sem=blk_recv,
                device_id=at(target), device_id_type=MESH,
            )

        @pl.when(dom == 1)
        def _():
            for x in range(cells_x):
                rows[x * cells_y : (x + 1) * cells_y, :] = divergence(x + WIDE)
            pieces = [None] * parts
            for y in range(cells_y):
                line = rows[pl.ds(y, cells_x, stride=cells_y), :]
                for p in range(parts):
                    by = ((y - p) * depth) % levels_z
                    moved = pltpu.roll(line, by, 1) if by else line
                    pieces[p] = moved if y == 0 else jnp.where(group == y, moved, pieces[p])
            for p in range(parts):
                block[p] = pieces[p]
            for i in range(1, count):
                block_copy(i).start()
            pltpu.make_async_copy(block.at[me // tiles_y], got.at[gy, gx], blk_recv).start()

        tab_x.wait()
        tab_y.wait()
        pltpu.make_async_copy(got, got, blk_recv).wait()
        highest = lax.Precision.HIGHEST
        for g in range(tiles_y):
            lines = got[g].reshape(total_x, levels_z)
            partly = jnp.dot(tx[...], lines, precision=highest, preferred_element_type=jnp.float32)
            turned[g * levels_z : (g + 1) * levels_z, :] = partly.T
        total_y = cells_y * tiles_y
        waves = total_x // tiles_y
        wide = 2 * waves
        each = levels_z // wide
        chunk = lax.broadcasted_iota(jnp.int32, (total_y, levels_z), 1) // wide
        for q in range(depth // each):
            packed = None
            for j in range(each):
                level = turned[pl.ds(q * each + j, total_y, stride=depth), :]
                packed = level if j == 0 else jnp.where(chunk == j, level, packed)
            both = jnp.dot(packed.T, ty[...], precision=highest, preferred_element_type=jnp.float32)
            for j in range(each):
                real = both[j * wide : j * wide + waves]
                imag = both[j * wide + waves : (j + 1) * wide]
                whole = real + pltpu.roll(imag, 2 * total_y, 1)
                spec_ref[0, q * each + j] = whole[:, :total_y]
                spec_ref[1, q * each + j] = whole[:, total_y : 2 * total_y]

        @pl.when(dom == 1)
        def _():
            for i in range(1, count):
                block_copy(i).wait_send()

    for copy in own:
        copy.wait_send()

    @pl.when(dom == 0)
    def _():
        for copy in inflow:
            copy.wait_send()
        block_in.wait_send()

    out.wait()


def tables(tiles_y, total_x, total_y, each):
    waves = total_x // tiles_y
    turn = 2.0 * np.pi / total_x * (np.outer(np.arange(total_x), np.arange(total_x)) % total_x)
    cosine, sine = np.cos(turn) / np.sqrt(total_x), -np.sin(turn) / np.sqrt(total_x)
    along = np.stack([cosine.reshape(tiles_y, waves, total_x), sine.reshape(tiles_y, waves, total_x)], 1)
    along = np.tile(along.reshape(tiles_y, 2 * waves, total_x), (1, each, 1))
    turn = 2.0 * np.pi / total_y * (np.outer(np.arange(total_y), np.arange(total_y)) % total_y)
    cosine, sine = np.cos(turn) / np.sqrt(total_y), np.sin(turn) / np.sqrt(total_y)
    across = np.concatenate([cosine, -sine, sine, cosine], 1)
    return along.astype(np.float32), across.astype(np.float32)


def on_device(tiles_x, tiles_y, velocity, fringe_start):
    _, _, cells_x, cells_y, levels_z = velocity.shape
    total_x, total_y = cells_x * tiles_x, cells_y * tiles_y
    fringe_len = min(8 * cells_x, total_x // 2)
    parts = 2 * tiles_x
    depth = levels_z // parts
    waves = total_x // tiles_y
    fused = cells_y * depth == levels_z and 4 * total_y == levels_z and 8 * waves == levels_z
    sizes = (tiles_x, tiles_y, cells_x, cells_y, levels_z, fringe_len)
    field = pltpu.VMEM((3, cells_x + 2 * WIDE, cells_y + 2 * BASE, levels_z), jnp.float32)
    strips = pltpu.VMEM((2, 3, cells_x, WIDE, levels_z), jnp.float32)
    corners = pltpu.VMEM((2, 2, 3, WIDE, WIDE, levels_z), jnp.float32)
    dma = pltpu.SemaphoreType.DMA
    scratch = [field] * 5 + [strips] * 3 + [corners] * 2
    scratch += [pltpu.VMEM((cells_x + 2 * WIDE, levels_z), jnp.float32)]
    scratch += [dma, dma((8,)), dma((8,)), dma((9,)), dma((9,)), dma]
    anywhere, vmem = pl.BlockSpec(memory_space=pl.ANY), pl.BlockSpec(memory_space=pltpu.VMEM)
    args = [fringe_start, velocity]
    in_specs = [pl.BlockSpec(memory_space=pltpu.SMEM), anywhere]
    if fused:
        along, across = tables(tiles_y, total_x, total_y, levels_z // (2 * waves))
        args += [jnp.asarray(along), jnp.asarray(across)]
        in_specs += [anywhere, anywhere]
        second = (2, depth, waves, total_y)
        scratch += [
            pltpu.VMEM(along.shape[1:], jnp.float32),
            pltpu.VMEM(across.shape, jnp.float32),
            pltpu.VMEM((cells_x * cells_y, levels_z), jnp.float32),
            pltpu.VMEM((parts, cells_x, levels_z), jnp.float32),
            pltpu.VMEM((tiles_y, tiles_x, cells_x, levels_z), jnp.float32),
            pltpu.VMEM((tiles_y * levels_z, levels_z), jnp.float32),
            dma((2,)), dma((parts * tiles_y,)), dma, dma,
        ]
    else:
        second = (cells_x, cells_y, levels_z)
    field_out, other = pl.pallas_call(
        functools.partial(step_kernel, sizes, fused),
        out_shape=(
            jax.ShapeDtypeStruct(velocity.shape, jnp.float32),
            jax.ShapeDtypeStruct(second, jnp.float32),
        ),
        in_specs=in_specs,
        out_specs=(anywhere, vmem),
        scratch_shapes=scratch,
        compiler_params=pltpu.CompilerParams(
            collective_id=0, has_side_effects=True, vmem_limit_bytes=32 * 1024 * 1024
        ),
        name="farm_step",
    )(*args)
    if fused:
        return field_out, other
    return field_out, spectrum_of(other)


def spectrum_of(divergence):
    cells_x, cells_y, levels_z = divergence.shape
    tiles_x = lax.axis_size("gx")
    total_x, total_y = cells_x * tiles_x, cells_y * lax.axis_size("gy")
    is_farm = lax.axis_index("dom") == 1
    levels_out = levels_z // (2 * tiles_x)
    tile_block = divergence.reshape(cells_x, cells_y, 2, tiles_x, levels_out)
    highest = lax.Precision.HIGHEST
    cos_table_x, sin_table_x = dft_tables(total_x)
    cos_table_y, sin_table_y = dft_tables(total_y)
    shard_piece = lax.all_to_all(tile_block, "gx", split_axis=3, concat_axis=0, tiled=True)
    real_part = jnp.einsum("xyhgc,xk->yhck", shard_piece, cos_table_x, precision=highest)
    imag_part = -jnp.einsum("xyhgc,xk->yhck", shard_piece, sin_table_x, precision=highest)
    real_part, imag_part = (real_part, imag_part)
    real_in = lax.all_to_all(real_part, "gy", split_axis=3, concat_axis=0, tiled=True)
    imag_in = lax.all_to_all(imag_part, "gy", split_axis=3, concat_axis=0, tiled=True)
    real_out = jnp.einsum("yhck,yj->hckj", real_in, cos_table_y, precision=highest) + jnp.einsum(
        "yhck,yj->hckj", imag_in, sin_table_y, precision=highest
    )
    imag_out = jnp.einsum("yhck,yj->hckj", imag_in, cos_table_y, precision=highest) - jnp.einsum(
        "yhck,yj->hckj", real_in, sin_table_y, precision=highest
    )
    packed = jnp.stack([real_out, imag_out])
    received = partner_half(packed[:, 0])
    spectrum = jnp.where(is_farm, packed[:, 1], received)
    return spectrum


def solution(mesh):
    in_specs = (P("dom", None, "gx", "gy", None), P())
    out_specs = (P("dom", None, "gx", "gy", None), P(None, ("dom", "gx"), "gy", None))
    return jax.shard_map(
        functools.partial(on_device, mesh.shape["gx"], mesh.shape["gy"]),
        mesh=mesh, in_specs=in_specs, out_specs=out_specs, check_vma=False,
    )
```

```python
import functools
import math

import jax
import jax.numpy as jnp
import numpy as np
from jax import lax
from jax.experimental import pallas as pl
from jax.experimental.pallas import tpu as pltpu
from jax.sharding import PartitionSpec as P

time_step = 0.1
fringe_rate = 1.0
smag_coef = 0.03
base_visc = 0.02
strain_floor = 0.25
MESH = pl.DeviceIdType.MESH
WIDE = 4
BASE = 8


def from_behind(shard, axis, by):
    peers = lax.axis_size(axis)
    pairs = [(i, i + by) for i in range(peers) if 0 <= i + by < peers]
    return lax.ppermute(shard, axis, pairs)


def partner_half(values):
    return from_behind(values, "dom", -1)


def dft_tables(length):
    positions = jnp.arange(length, dtype=jnp.int32)
    phase = (positions[:, None] * positions[None, :] % length).astype(jnp.float32) * (
        2.0 * math.pi / length
    )
    factor = 1.0 / math.sqrt(length)
    return (jnp.cos(phase) * factor, jnp.sin(phase) * factor)


def step_kernel(sizes, fused, *refs):
    tiles_x, tiles_y, cells_x, cells_y, levels_z, fringe_len = sizes
    if fused:
        (fs_ref, u_hbm, tx_hbm, ty_hbm, v_hbm, spec_ref, *scratch) = refs
    else:
        (fs_ref, u_hbm, v_hbm, div_ref, *scratch) = refs
    (U, I, S1, S2, S3, edge, near, near_in, tips, diag, diag_in, ramp) = scratch[:12]
    (load_sem, send_sem, recv_sem, in_send, in_recv, out_sem) = scratch[12:18]
    if fused:
        tx, ty, rows, block, got, turned, tab_sem, blk_send, blk_recv = scratch[18:]
    dom, gx, gy = (lax.axis_index(name) for name in ("dom", "gx", "gy"))
    count = 2 * tiles_x * tiles_y
    me = (dom * tiles_x + gx) * tiles_y + gy
    total_x = cells_x * tiles_x
    hi = WIDE + cells_x
    inner = pl.ds(BASE, cells_y)

    def at(index):
        return (
            index // (tiles_x * tiles_y),
            lax.rem(index // tiles_y, tiles_x),
            lax.rem(index, tiles_y),
        )

    def beside(domain, dx, dy):
        return (
            domain,
            lax.rem(gx + dx + tiles_x, tiles_x),
            lax.rem(gy + dy + tiles_y, tiles_y),
        )

    around = [(1, 0), (-1, 0), (0, 1), (0, -1), (1, 1), (1, -1), (-1, 1), (-1, -1)]
    barrier = pltpu.get_barrier_semaphore()
    if fused:
        @pl.loop(1, count)
        def _(i):
            pl.semaphore_signal(
                barrier, inc=1, device_id=at(lax.rem(me + i, count)), device_id_type=MESH
            )
    else:
        for dx, dy in around:
            for domain in range(2):
                pl.semaphore_signal(
                    barrier, inc=1, device_id=beside(domain, dx, dy), device_id_type=MESH
                )
        pl.semaphore_signal(barrier, inc=1, device_id=beside(1 - dom, 0, 0), device_id_type=MESH)

    load = pltpu.make_async_copy(u_hbm.at[0], U.at[:, pl.ds(WIDE, cells_x), inner, :], load_sem)
    load.start()
    if fused:
        tab_x = pltpu.make_async_copy(tx_hbm.at[gy], tx, tab_sem.at[0])
        tab_y = pltpu.make_async_copy(ty_hbm, ty, tab_sem.at[1])
        tab_x.start()
        tab_y.start()

    cell = lax.broadcasted_iota(jnp.int32, ramp.shape, 0) + (gx * cells_x - WIDE)
    offset = cell - fs_ref[0]
    for _ in range(2):
        offset = jnp.where(offset < 0, offset + total_x, offset)
    offset = jnp.where(offset >= total_x, offset - total_x, offset)
    sine = jnp.sin((offset.astype(jnp.float32) + 0.5) * (math.pi / fringe_len))
    farm = dom.astype(jnp.float32)
    ramp[...] = jnp.where(offset < fringe_len, fringe_rate * sine * sine, 0.0) * farm

    @pl.when(dom == 0)
    def _():
        I[...] = jnp.zeros_like(I)

    load.wait()
    for side in range(2):
        start = BASE if side == 0 else BASE + cells_y - WIDE
        for c in range(3):
            for j in range(WIDE):
                edge[side, c, j] = U[c, WIDE:hi, start + j, :]
        tips[0, side] = U[:, hi - WIDE : hi, start : start + WIDE, :]
        tips[1, side] = U[:, WIDE : 2 * WIDE, start : start + WIDE, :]
    pl.semaphore_wait(barrier, count - 1 if fused else 17)

    def margins(domain, field, strips, corners, sends, recvs, width):
        low, high = pl.ds(WIDE - width, width), pl.ds(hi, width)
        less = width - 1
        pieces = []
        for dx, dy in around:
            mine = pl.ds(hi - width, width) if dx > 0 else pl.ds(WIDE, width)
            side = 1 if dy > 0 else 0
            span = pl.ds(WIDE - width if dy > 0 else 0, width)
            if dy == 0:
                pieces.append((U.at[:, mine, inner, :], field.at[:, low if dx > 0 else high, inner, :]))
            elif dx == 0:
                pieces.append((edge.at[side, :, span], strips.at[1 - side, :, span]))
            else:
                part = pl.ds(WIDE - less if dx > 0 else 0, less)
                pieces.append((
                    tips.at[0 if dx > 0 else 1, side, :, part],
                    corners.at[0 if dx > 0 else 1, 1 - side, :, part],
                ))
        return [
            pltpu.make_async_remote_copy(
                src_ref=source, dst_ref=target, send_sem=sends.at[i], recv_sem=recvs.at[i],
                device_id=beside(domain, *around[i]), device_id_type=MESH,
            )
            for i, (source, target) in enumerate(pieces)
        ]

    def place(field, strips, corners):
        for side in range(2):
            start = BASE - WIDE if side == 0 else BASE + cells_y
            span = pl.ds(start, WIDE)
            for c in range(3):
                for j in range(WIDE):
                    field[c, WIDE:hi, start + j, :] = strips[side, c, j]
            field[:, 0:WIDE, span, :] = corners[0, side]
            field[:, hi : hi + WIDE, span, :] = corners[1, side]

    to_pre = margins(0, U, near, diag, send_sem, recv_sem, WIDE - 1)
    to_farm = margins(1, U, near, diag, send_sem, recv_sem, WIDE)
    inflow = margins(1, I, near_in, diag_in, in_send, in_recv, WIDE - 1)
    block_in = pltpu.make_async_remote_copy(
        src_ref=U.at[:, pl.ds(WIDE, cells_x), inner, :],
        dst_ref=I.at[:, pl.ds(WIDE, cells_x), inner, :],
        send_sem=in_send.at[8], recv_sem=in_recv.at[8],
        device_id=(1 - dom, gx, gy), device_id_type=MESH,
    )
    order = [2, 3, 4, 5, 6, 7, 0, 1]

    @pl.when(dom == 0)
    def _():
        for i in order:
            to_pre[i].start()
        for i in order:
            inflow[i].start()
        block_in.start()
        for copy in to_pre:
            copy.wait_recv()
        place(U, near, diag)

    @pl.when(dom == 1)
    def _():
        for i in order:
            to_farm[i].start()
        for copy in to_farm:
            copy.wait_recv()
        place(U, near, diag)
        for copy in inflow:
            copy.wait_recv()
        block_in.wait_recv()
        place(I, near_in, diag_in)

    lane = lax.broadcasted_iota(jnp.int32, (8, levels_z), 1)
    first, last = lane == 0, lane == levels_z - 1

    def rate(field, x, row):
        centre = [field[c, x, pl.ds(row, 8), :] for c in range(3)]
        grads, laps = [[], [], []], []
        for c in range(3):
            xp, xm = field[c, x + 1, pl.ds(row, 8), :], field[c, x - 1, pl.ds(row, 8), :]
            yp, ym = field[c, x, pl.ds(row + 1, 8), :], field[c, x, pl.ds(row - 1, 8), :]
            zp = jnp.where(last, 0.0, pltpu.roll(centre[c], levels_z - 1, 1))
            zm = jnp.where(first, 0.0, pltpu.roll(centre[c], 1, 1))
            grads[0].append(xp - xm)
            grads[1].append(yp - ym)
            grads[2].append(zp - zm)
            laps.append((xp + xm) + (yp + ym) + (zp + zm) - 6.0 * centre[c])
        (axx, axy, axz), (ayx, ayy, ayz), (azx, azy, azz) = grads
        shear = (axy + ayx, axz + azx, ayz + azy)
        diagonal = axx * axx + ayy * ayy + azz * azz
        sheared = shear[0] * shear[0] + shear[1] * shear[1] + shear[2] * shear[2]
        under = 0.5 * diagonal + (0.25 * sheared + strain_floor)
        eddy = base_visc + smag_coef * (under * lax.rsqrt(under))
        pull = jnp.broadcast_to(ramp[pl.ds(x, 1), :], (8, levels_z))
        rates = []
        for c in range(3):
            carried = centre[0] * grads[0][c] + centre[1] * grads[1][c] + centre[2] * grads[2][c]
            behind = I[c, x, pl.ds(row, 8), :] - centre[c]
            rates.append(eddy * laps[c] - 0.5 * carried + pull * behind)
        return centre, rates

    def stage(field, result, margin, finish):
        starts = (BASE - margin, BASE + cells_y + margin - 8)

        @pl.loop(WIDE - margin, hi + margin, unroll=cells_x + 2 * margin)
        def _(x):
            for row in starts:
                centre, rates = rate(field, x, row)
                for c in range(3):
                    result[c, x, pl.ds(row, 8), :] = finish(
                        U[c, x, pl.ds(row, 8), :], centre[c] + time_step * rates[c]
                    )

    stage(U, S1, 3, lambda start, moved: moved)
    stage(S1, S2, 2, lambda start, moved: 0.75 * start + 0.25 * moved)
    stage(S2, S3, 1, lambda start, moved: (1.0 / 3.0) * start + (2.0 / 3.0) * moved)

    out = pltpu.make_async_copy(S3.at[:, pl.ds(WIDE, cells_x), inner, :], v_hbm.at[0], out_sem)
    out.start()

    def divergence(x):
        w = S3[2, x, inner, :]
        up = jnp.where(last, 0.0, pltpu.roll(w, levels_z - 1, 1))
        down = jnp.where(first, 0.0, pltpu.roll(w, 1, 1))
        along = 0.5 * (S3[0, x + 1, inner, :] - S3[0, x - 1, inner, :])
        across = 0.5 * (S3[1, x, pl.ds(BASE + 1, 8), :] - S3[1, x, pl.ds(BASE - 1, 8), :])
        return along + across + 0.5 * (up - down)

    if not fused:
        for x in range(cells_x):
            div_ref[x] = divergence(x + WIDE)
    else:
        parts = 2 * tiles_x
        depth = levels_z // parts
        group = lax.broadcasted_iota(jnp.int32, (cells_x, levels_z), 1) // depth

        def block_copy(i):
            target = lax.rem(me + i, count)
            return pltpu.make_async_remote_copy(
                src_ref=block.at[target // tiles_y], dst_ref=got.at[gy, gx],
                send_sem=blk_send.at[i], recv_sem=blk_recv,
                device_id=at(target), device_id_type=MESH,
            )

        @pl.when(dom == 1)
        def _():
            for x in range(cells_x):
                rows[x * cells_y : (x + 1) * cells_y, :] = divergence(x + WIDE)
            pieces = [None] * parts
            for y in range(cells_y):
                line = rows[pl.ds(y, cells_x, stride=cells_y), :]
                for p in range(parts):
                    by = ((y - p) * depth) % levels_z
                    moved = pltpu.roll(line, by, 1) if by else line
                    pieces[p] = moved if y == 0 else jnp.where(group == y, moved, pieces[p])
            for p in range(parts):
                block[p] = pieces[p]
            for i in range(1, count):
                block_copy(i).start()
            pltpu.make_async_copy(block.at[me // tiles_y], got.at[gy, gx], blk_recv).start()

        tab_x.wait()
        tab_y.wait()
        pltpu.make_async_copy(got, got, blk_recv).wait()
        highest = lax.Precision.HIGHEST
        for g in range(tiles_y):
            lines = got[g].reshape(total_x, levels_z)
            partly = jnp.dot(tx[...], lines, precision=highest, preferred_element_type=jnp.float32)
            turned[g * levels_z : (g + 1) * levels_z, :] = partly.T
        total_y = cells_y * tiles_y
        waves = total_x // tiles_y
        wide = 2 * waves
        each = levels_z // wide
        chunk = lax.broadcasted_iota(jnp.int32, (total_y, levels_z), 1) // wide
        for q in range(depth // each):
            packed = None
            for j in range(each):
                level = turned[pl.ds(q * each + j, total_y, stride=depth), :]
                packed = level if j == 0 else jnp.where(chunk == j, level, packed)
            both = jnp.dot(packed.T, ty[...], precision=highest, preferred_element_type=jnp.float32)
            for j in range(each):
                real = both[j * wide : j * wide + waves]
                imag = both[j * wide + waves : (j + 1) * wide]
                whole = real + pltpu.roll(imag, 2 * total_y, 1)
                spec_ref[0, q * each + j] = whole[:, :total_y]
                spec_ref[1, q * each + j] = whole[:, total_y : 2 * total_y]

        @pl.when(dom == 1)
        def _():
            for i in range(1, count):
                block_copy(i).wait_send()

    @pl.when(dom == 1)
    def _():
        for copy in to_farm:
            copy.wait_send()

    @pl.when(dom == 0)
    def _():
        for copy in to_pre + inflow:
            copy.wait_send()
        block_in.wait_send()

    out.wait()


def tables(tiles_y, total_x, total_y, each):
    waves = total_x // tiles_y
    turn = 2.0 * np.pi / total_x * (np.outer(np.arange(total_x), np.arange(total_x)) % total_x)
    cosine, sine = np.cos(turn) / np.sqrt(total_x), -np.sin(turn) / np.sqrt(total_x)
    along = np.stack([cosine.reshape(tiles_y, waves, total_x), sine.reshape(tiles_y, waves, total_x)], 1)
    along = np.tile(along.reshape(tiles_y, 2 * waves, total_x), (1, each, 1))
    turn = 2.0 * np.pi / total_y * (np.outer(np.arange(total_y), np.arange(total_y)) % total_y)
    cosine, sine = np.cos(turn) / np.sqrt(total_y), np.sin(turn) / np.sqrt(total_y)
    across = np.concatenate([cosine, -sine, sine, cosine], 1)
    return along.astype(np.float32), across.astype(np.float32)


def on_device(tiles_x, tiles_y, velocity, fringe_start):
    _, _, cells_x, cells_y, levels_z = velocity.shape
    total_x, total_y = cells_x * tiles_x, cells_y * tiles_y
    fringe_len = min(8 * cells_x, total_x // 2)
    parts = 2 * tiles_x
    depth = levels_z // parts
    waves = total_x // tiles_y
    fused = cells_y * depth == levels_z and 4 * total_y == levels_z and 8 * waves == levels_z
    sizes = (tiles_x, tiles_y, cells_x, cells_y, levels_z, fringe_len)
    field = pltpu.VMEM((3, cells_x + 2 * WIDE, cells_y + 2 * BASE, levels_z), jnp.float32)
    strips = pltpu.VMEM((2, 3, WIDE, cells_x, levels_z), jnp.float32)
    corners = pltpu.VMEM((2, 2, 3, WIDE, WIDE, levels_z), jnp.float32)
    dma = pltpu.SemaphoreType.DMA
    scratch = [field] * 5 + [strips] * 3 + [corners] * 3
    scratch += [pltpu.VMEM((cells_x + 2 * WIDE, levels_z), jnp.float32)]
    scratch += [dma, dma((8,)), dma((8,)), dma((9,)), dma((9,)), dma]
    anywhere, vmem = pl.BlockSpec(memory_space=pltpu.HBM), pl.BlockSpec(memory_space=pltpu.VMEM)
    args = [fringe_start, velocity]
    in_specs = [pl.BlockSpec(memory_space=pltpu.SMEM), anywhere]
    if fused:
        along, across = tables(tiles_y, total_x, total_y, levels_z // (2 * waves))
        args += [jnp.asarray(along), jnp.asarray(across)]
        in_specs += [anywhere, anywhere]
        second = (2, depth, waves, total_y)
        scratch += [
            pltpu.VMEM(along.shape[1:], jnp.float32),
            pltpu.VMEM(across.shape, jnp.float32),
            pltpu.VMEM((cells_x * cells_y, levels_z), jnp.float32),
            pltpu.VMEM((parts, cells_x, levels_z), jnp.float32),
            pltpu.VMEM((tiles_y, tiles_x, cells_x, levels_z), jnp.float32),
            pltpu.VMEM((tiles_y * levels_z, levels_z), jnp.float32),
            dma((2,)), dma((parts * tiles_y,)), dma,
        ]
    else:
        second = (cells_x, cells_y, levels_z)
    field_out, other = pl.pallas_call(
        functools.partial(step_kernel, sizes, fused),
        out_shape=(
            jax.ShapeDtypeStruct(velocity.shape, jnp.float32),
            jax.ShapeDtypeStruct(second, jnp.float32),
        ),
        in_specs=in_specs,
        out_specs=(anywhere, vmem),
        scratch_shapes=scratch,
        compiler_params=pltpu.CompilerParams(
            collective_id=0, has_side_effects=True, vmem_limit_bytes=60 * 1024 * 1024
        ),
        name="farm_step",
    )(*args)
    if fused:
        return field_out, other
    return field_out, spectrum_of(other)


def spectrum_of(divergence):
    cells_x, cells_y, levels_z = divergence.shape
    tiles_x = lax.axis_size("gx")
    total_x, total_y = cells_x * tiles_x, cells_y * lax.axis_size("gy")
    is_farm = lax.axis_index("dom") == 1
    levels_out = levels_z // (2 * tiles_x)
    tile_block = divergence.reshape(cells_x, cells_y, 2, tiles_x, levels_out)
    highest = lax.Precision.HIGHEST
    cos_table_x, sin_table_x = dft_tables(total_x)
    cos_table_y, sin_table_y = dft_tables(total_y)
    shard_piece = lax.all_to_all(tile_block, "gx", split_axis=3, concat_axis=0, tiled=True)
    real_part = jnp.einsum("xyhgc,xk->yhck", shard_piece, cos_table_x, precision=highest)
    imag_part = -jnp.einsum("xyhgc,xk->yhck", shard_piece, sin_table_x, precision=highest)
    real_part, imag_part = (real_part, imag_part)
    real_in = lax.all_to_all(real_part, "gy", split_axis=3, concat_axis=0, tiled=True)
    imag_in = lax.all_to_all(imag_part, "gy", split_axis=3, concat_axis=0, tiled=True)
    real_out = jnp.einsum("yhck,yj->hckj", real_in, cos_table_y, precision=highest) + jnp.einsum(
        "yhck,yj->hckj", imag_in, sin_table_y, precision=highest
    )
    imag_out = jnp.einsum("yhck,yj->hckj", imag_in, cos_table_y, precision=highest) - jnp.einsum(
        "yhck,yj->hckj", real_in, sin_table_y, precision=highest
    )
    packed = jnp.stack([real_out, imag_out])
    received = partner_half(packed[:, 0])
    spectrum = jnp.where(is_farm, packed[:, 1], received)
    return spectrum


def solution(mesh):
    in_specs = (P("dom", None, "gx", "gy", None), P())
    out_specs = (P("dom", None, "gx", "gy", None), P(None, ("dom", "gx"), "gy", None))
    return jax.shard_map(
        functools.partial(on_device, mesh.shape["gx"], mesh.shape["gy"]),
        mesh=mesh, in_specs=in_specs, out_specs=out_specs, check_vma=False,
    )
```

```python
import functools
import math

import jax
import jax.numpy as jnp
import numpy as np
from jax import lax
from jax.experimental import pallas as pl
from jax.experimental.pallas import tpu as pltpu
from jax.sharding import PartitionSpec as P

time_step = 0.1
fringe_rate = 1.0
smag_coef = 0.03
base_visc = 0.02
strain_floor = 0.25
MESH = pl.DeviceIdType.MESH
WIDE = 4
BASE = 8


def from_behind(shard, axis, by):
    peers = lax.axis_size(axis)
    pairs = [(i, i + by) for i in range(peers) if 0 <= i + by < peers]
    return lax.ppermute(shard, axis, pairs)


def partner_half(values):
    return from_behind(values, "dom", -1)


def dft_tables(length):
    positions = jnp.arange(length, dtype=jnp.int32)
    phase = (positions[:, None] * positions[None, :] % length).astype(jnp.float32) * (
        2.0 * math.pi / length
    )
    factor = 1.0 / math.sqrt(length)
    return (jnp.cos(phase) * factor, jnp.sin(phase) * factor)


def step_kernel(sizes, fused, *refs):
    tiles_x, tiles_y, cells_x, cells_y, levels_z, fringe_len = sizes
    if fused:
        (fs_ref, u_hbm, v_hbm, got, *scratch) = refs
    else:
        (fs_ref, u_hbm, v_hbm, div_ref, *scratch) = refs
    (U, I, S1, S2, S3, edge, near, near_in, tips, diag, diag_in, ramp) = scratch[:12]
    (load_sem, send_sem, recv_sem, in_send, in_recv, out_sem) = scratch[12:18]
    if fused:
        rows, block, blk_send, blk_recv = scratch[18:]
    dom, gx, gy = (lax.axis_index(name) for name in ("dom", "gx", "gy"))
    count = 2 * tiles_x * tiles_y
    me = (dom * tiles_x + gx) * tiles_y + gy
    total_x = cells_x * tiles_x
    hi = WIDE + cells_x
    inner = pl.ds(BASE, cells_y)

    def at(index):
        return (
            index // (tiles_x * tiles_y),
            lax.rem(index // tiles_y, tiles_x),
            lax.rem(index, tiles_y),
        )

    def beside(domain, dx, dy):
        return (
            domain,
            lax.rem(gx + dx + tiles_x, tiles_x),
            lax.rem(gy + dy + tiles_y, tiles_y),
        )

    around = [(1, 0), (-1, 0), (0, 1), (0, -1), (1, 1), (1, -1), (-1, 1), (-1, -1)]
    barrier = pltpu.get_barrier_semaphore()
    if fused:
        @pl.loop(1, count)
        def _(i):
            pl.semaphore_signal(
                barrier, inc=1, device_id=at(lax.rem(me + i, count)), device_id_type=MESH
            )
    else:
        for dx, dy in around:
            for domain in range(2):
                pl.semaphore_signal(
                    barrier, inc=1, device_id=beside(domain, dx, dy), device_id_type=MESH
                )
        pl.semaphore_signal(barrier, inc=1, device_id=beside(1 - dom, 0, 0), device_id_type=MESH)

    load = pltpu.make_async_copy(u_hbm.at[0], U.at[:, pl.ds(WIDE, cells_x), inner, :], load_sem)
    load.start()

    cell = lax.broadcasted_iota(jnp.int32, ramp.shape, 0) + (gx * cells_x - WIDE)
    offset = cell - fs_ref[0]
    for _ in range(2):
        offset = jnp.where(offset < 0, offset + total_x, offset)
    offset = jnp.where(offset >= total_x, offset - total_x, offset)
    sine = jnp.sin((offset.astype(jnp.float32) + 0.5) * (math.pi / fringe_len))
    farm = dom.astype(jnp.float32)
    ramp[...] = jnp.where(offset < fringe_len, fringe_rate * sine * sine, 0.0) * farm

    @pl.when(dom == 0)
    def _():
        I[...] = jnp.zeros_like(I)

    load.wait()
    for side in range(2):
        start = BASE if side == 0 else BASE + cells_y - WIDE
        for c in range(3):
            for j in range(WIDE):
                edge[side, c, j] = U[c, WIDE:hi, start + j, :]
        tips[0, side] = U[:, hi - WIDE : hi, start : start + WIDE, :]
        tips[1, side] = U[:, WIDE : 2 * WIDE, start : start + WIDE, :]
    pl.semaphore_wait(barrier, count - 1 if fused else 17)

    def margins(domain, field, strips, corners, sends, recvs, width):
        low, high = pl.ds(WIDE - width, width), pl.ds(hi, width)
        less = width - 1
        pieces = []
        for dx, dy in around:
            mine = pl.ds(hi - width, width) if dx > 0 else pl.ds(WIDE, width)
            side = 1 if dy > 0 else 0
            span = pl.ds(WIDE - width if dy > 0 else 0, width)
            if dy == 0:
                pieces.append((U.at[:, mine, inner, :], field.at[:, low if dx > 0 else high, inner, :]))
            elif dx == 0:
                pieces.append((edge.at[side, :, span], strips.at[1 - side, :, span]))
            else:
                part = pl.ds(WIDE - less if dx > 0 else 0, less)
                pieces.append((
                    tips.at[0 if dx > 0 else 1, side, :, part],
                    corners.at[0 if dx > 0 else 1, 1 - side, :, part],
                ))
        return [
            pltpu.make_async_remote_copy(
                src_ref=source, dst_ref=target, send_sem=sends.at[i], recv_sem=recvs.at[i],
                device_id=beside(domain, *around[i]), device_id_type=MESH,
            )
            for i, (source, target) in enumerate(pieces)
        ]

    def onward(width):
        less = width - 1
        pairs = []
        for dx, dy in around:
            side = 0 if dy > 0 else 1
            span = pl.ds(WIDE - width if dy > 0 else 0, width)
            slab = pl.ds(WIDE - width if dx > 0 else hi, width)
            part = (0 if dx > 0 else 1, side, slice(None), pl.ds(WIDE - less if dx > 0 else 0, less))
            if dy == 0:
                pairs.append((U.at[:, slab, inner, :], I.at[:, slab, inner, :]))
            elif dx == 0:
                pairs.append((near.at[side, :, span], near_in.at[side, :, span]))
            else:
                pairs.append((diag.at[part], diag_in.at[part]))
        return [
            pltpu.make_async_remote_copy(
                src_ref=source, dst_ref=target, send_sem=in_send.at[i], recv_sem=in_recv.at[i],
                device_id=(1 - dom, gx, gy), device_id_type=MESH,
            )
            for i, (source, target) in enumerate(pairs)
        ]

    def place(field, strips, corners):
        for side in range(2):
            start = BASE - WIDE if side == 0 else BASE + cells_y
            span = pl.ds(start, WIDE)
            for c in range(3):
                for j in range(WIDE):
                    field[c, WIDE:hi, start + j, :] = strips[side, c, j]
            field[:, 0:WIDE, span, :] = corners[0, side]
            field[:, hi : hi + WIDE, span, :] = corners[1, side]

    to_pre = margins(0, U, near, diag, send_sem, recv_sem, WIDE - 1)
    to_farm = margins(1, U, near, diag, send_sem, recv_sem, WIDE)
    inflow = onward(WIDE - 1)
    block_in = pltpu.make_async_remote_copy(
        src_ref=U.at[:, pl.ds(WIDE, cells_x), inner, :],
        dst_ref=I.at[:, pl.ds(WIDE, cells_x), inner, :],
        send_sem=in_send.at[8], recv_sem=in_recv.at[8],
        device_id=(1 - dom, gx, gy), device_id_type=MESH,
    )
    order = [2, 3, 4, 5, 6, 7, 0, 1]

    @pl.when(dom == 0)
    def _():
        for i in order:
            to_pre[i].start()
        block_in.start()
        for i in order:
            to_pre[i].wait_recv()
            inflow[i].start()
        place(U, near, diag)

    @pl.when(dom == 1)
    def _():
        for i in order:
            to_farm[i].start()
        for copy in to_farm:
            copy.wait_recv()
        place(U, near, diag)

    lane = lax.broadcasted_iota(jnp.int32, (8, levels_z), 1)
    first, last = lane == 0, lane == levels_z - 1

    def rate(field, x, row, pulled=True):
        centre = [field[c, x, pl.ds(row, 8), :] for c in range(3)]
        grads, laps = [[], [], []], []
        for c in range(3):
            xp, xm = field[c, x + 1, pl.ds(row, 8), :], field[c, x - 1, pl.ds(row, 8), :]
            yp, ym = field[c, x, pl.ds(row + 1, 8), :], field[c, x, pl.ds(row - 1, 8), :]
            zp = jnp.where(last, 0.0, pltpu.roll(centre[c], levels_z - 1, 1))
            zm = jnp.where(first, 0.0, pltpu.roll(centre[c], 1, 1))
            grads[0].append(xp - xm)
            grads[1].append(yp - ym)
            grads[2].append(zp - zm)
            laps.append((xp + xm) + (yp + ym) + (zp + zm) - 6.0 * centre[c])
        (axx, axy, axz), (ayx, ayy, ayz), (azx, azy, azz) = grads
        shear = (axy + ayx, axz + azx, ayz + azy)
        diagonal = axx * axx + ayy * ayy + azz * azz
        sheared = shear[0] * shear[0] + shear[1] * shear[1] + shear[2] * shear[2]
        under = 0.5 * diagonal + (0.25 * sheared + strain_floor)
        eddy = base_visc + smag_coef * (under * lax.rsqrt(under))
        pull = jnp.broadcast_to(ramp[pl.ds(x, 1), :], (8, levels_z))
        rates = []
        for c in range(3):
            carried = centre[0] * grads[0][c] + centre[1] * grads[1][c] + centre[2] * grads[2][c]
            free = eddy * laps[c] - 0.5 * carried
            if pulled:
                free = free + pull * (I[c, x, pl.ds(row, 8), :] - centre[c])
            rates.append(free)
        return centre, rates

    def stage(field, result, margin, finish, pulled=True):
        starts = (BASE - margin, BASE + cells_y + margin - 8)

        @pl.loop(WIDE - margin, hi + margin, unroll=cells_x + 2 * margin)
        def _(x):
            for row in starts:
                centre, rates = rate(field, x, row, pulled)
                for c in range(3):
                    result[c, x, pl.ds(row, 8), :] = finish(
                        U[c, x, pl.ds(row, 8), :], centre[c] + time_step * rates[c]
                    )

    stage(U, S1, 3, lambda start, moved: moved, pulled=False)

    @pl.when(dom == 1)
    def _():
        for copy in inflow:
            copy.wait_recv()
        block_in.wait_recv()
        place(I, near_in, diag_in)

        @pl.loop(WIDE - 3, hi + 3, unroll=2)
        def _(x):
            pull = time_step * jnp.broadcast_to(ramp[pl.ds(x, 1), :], (8, levels_z))
            for row in (BASE - 3, BASE + 5):
                for c in range(3):
                    S1[c, x, pl.ds(row, 8), :] += pull * (
                        I[c, x, pl.ds(row, 8), :] - U[c, x, pl.ds(row, 8), :]
                    )

    stage(S1, S2, 2, lambda start, moved: 0.75 * start + 0.25 * moved)
    stage(S2, S3, 1, lambda start, moved: (1.0 / 3.0) * start + (2.0 / 3.0) * moved)

    out = pltpu.make_async_copy(S3.at[:, pl.ds(WIDE, cells_x), inner, :], v_hbm.at[0], out_sem)
    out.start()

    def divergence(x):
        w = S3[2, x, inner, :]
        up = jnp.where(last, 0.0, pltpu.roll(w, levels_z - 1, 1))
        down = jnp.where(first, 0.0, pltpu.roll(w, 1, 1))
        along = 0.5 * (S3[0, x + 1, inner, :] - S3[0, x - 1, inner, :])
        across = 0.5 * (S3[1, x, pl.ds(BASE + 1, 8), :] - S3[1, x, pl.ds(BASE - 1, 8), :])
        return along + across + 0.5 * (up - down)

    if not fused:
        for x in range(cells_x):
            div_ref[x] = divergence(x + WIDE)
    else:
        parts = 2 * tiles_x
        depth = levels_z // parts
        group = lax.broadcasted_iota(jnp.int32, (cells_x, levels_z), 1) // depth

        def block_copy(i):
            target = lax.rem(me + i, count)
            return pltpu.make_async_remote_copy(
                src_ref=block.at[target // tiles_y], dst_ref=got.at[gy, gx],
                send_sem=blk_send.at[i], recv_sem=blk_recv,
                device_id=at(target), device_id_type=MESH,
            )

        @pl.when(dom == 1)
        def _():
            for x in range(cells_x):
                rows[x * cells_y : (x + 1) * cells_y, :] = divergence(x + WIDE)
            pieces = [None] * parts
            for y in range(cells_y):
                line = rows[pl.ds(y, cells_x, stride=cells_y), :]
                for p in range(parts):
                    by = ((y - p) * depth) % levels_z
                    moved = pltpu.roll(line, by, 1) if by else line
                    pieces[p] = moved if y == 0 else jnp.where(group == y, moved, pieces[p])
            for p in range(parts):
                block[p] = pieces[p]
            for i in range(1, count):
                block_copy(i).start()
            pltpu.make_async_copy(block.at[me // tiles_y], got.at[gy, gx], blk_recv).start()

        pltpu.make_async_copy(got, got, blk_recv).wait()

        @pl.when(dom == 1)
        def _():
            for i in range(1, count):
                block_copy(i).wait_send()

    @pl.when(dom == 1)
    def _():
        for copy in to_farm:
            copy.wait_send()

    @pl.when(dom == 0)
    def _():
        for copy in to_pre + inflow:
            copy.wait_send()
        block_in.wait_send()

    out.wait()


def transform_kernel(
    sizes, got_hbm, tx_hbm, ty_hbm, v_from, v_hbm, spec_hbm, spec_ref, turned, got, tx, ty, v_ref, sems
):
    tiles_x, tiles_y, cells_x, cells_y, levels_z, _ = sizes
    gy = lax.axis_index("gy")
    total_x = cells_x * tiles_x
    depth = levels_z // (2 * tiles_x)
    loads = [
        pltpu.make_async_copy(source, target, sems.at[i + 2])
        for i, (source, target) in enumerate(
            [(got_hbm, got), (tx_hbm.at[gy], tx), (ty_hbm, ty), (v_from, v_ref)]
        )
    ]
    for load in loads:
        load.start()
    save = pltpu.make_async_copy(v_ref, v_hbm, sems.at[0])
    for load in loads[:3]:
        load.wait()
    highest = lax.Precision.HIGHEST
    for g in range(tiles_y):
        lines = got[g].reshape(total_x, levels_z)
        partly = jnp.dot(tx[...], lines, precision=highest, preferred_element_type=jnp.float32)
        turned[g * levels_z : (g + 1) * levels_z, :] = partly.T
    total_y = cells_y * tiles_y
    waves = total_x // tiles_y
    wide = 2 * waves
    each = levels_z // wide
    chunk = lax.broadcasted_iota(jnp.int32, (total_y, levels_z), 1) // wide
    loads[3].wait()
    save.start()
    for q in range(depth // each):
        packed = None
        for j in range(each):
            level = turned[pl.ds(q * each + j, total_y, stride=depth), :]
            packed = level if j == 0 else jnp.where(chunk == j, level, packed)
        both = jnp.dot(packed.T, ty[...], precision=highest, preferred_element_type=jnp.float32)
        for j in range(each):
            real = both[j * wide : j * wide + waves]
            imag = both[j * wide + waves : (j + 1) * wide]
            whole = real + pltpu.roll(imag, 2 * total_y, 1)
            spec_ref[0, q * each + j] = whole[:, :total_y]
            spec_ref[1, q * each + j] = whole[:, total_y : 2 * total_y]
    store = pltpu.make_async_copy(spec_ref, spec_hbm, sems.at[1])
    store.start()
    store.wait()
    save.wait()


def tables(tiles_y, total_x, total_y, each):
    waves = total_x // tiles_y
    turn = 2.0 * np.pi / total_x * (np.outer(np.arange(total_x), np.arange(total_x)) % total_x)
    cosine, sine = np.cos(turn) / np.sqrt(total_x), -np.sin(turn) / np.sqrt(total_x)
    along = np.stack([cosine.reshape(tiles_y, waves, total_x), sine.reshape(tiles_y, waves, total_x)], 1)
    along = np.tile(along.reshape(tiles_y, 2 * waves, total_x), (1, each, 1))
    turn = 2.0 * np.pi / total_y * (np.outer(np.arange(total_y), np.arange(total_y)) % total_y)
    cosine, sine = np.cos(turn) / np.sqrt(total_y), np.sin(turn) / np.sqrt(total_y)
    across = np.concatenate([cosine, -sine, sine, cosine], 1)
    return along.astype(np.float32), across.astype(np.float32)


def on_device(tiles_x, tiles_y, velocity, fringe_start):
    _, _, cells_x, cells_y, levels_z = velocity.shape
    total_x, total_y = cells_x * tiles_x, cells_y * tiles_y
    fringe_len = min(8 * cells_x, total_x // 2)
    parts = 2 * tiles_x
    depth = levels_z // parts
    waves = total_x // tiles_y
    fused = cells_y * depth == levels_z and 4 * total_y == levels_z and 8 * waves == levels_z
    sizes = (tiles_x, tiles_y, cells_x, cells_y, levels_z, fringe_len)
    field = pltpu.VMEM((3, cells_x + 2 * WIDE, cells_y + 2 * BASE, levels_z), jnp.float32)
    strips = pltpu.VMEM((2, 3, WIDE, cells_x, levels_z), jnp.float32)
    corners = pltpu.VMEM((2, 2, 3, WIDE, WIDE, levels_z), jnp.float32)
    dma = pltpu.SemaphoreType.DMA
    scratch = [field] * 5 + [strips] * 3 + [corners] * 3
    scratch += [pltpu.VMEM((cells_x + 2 * WIDE, levels_z), jnp.float32)]
    scratch += [dma, dma((8,)), dma((8,)), dma((9,)), dma((9,)), dma]
    anywhere, vmem = pl.BlockSpec(memory_space=pltpu.HBM), pl.BlockSpec(memory_space=pltpu.VMEM)
    args = [fringe_start, velocity]
    in_specs = [pl.BlockSpec(memory_space=pltpu.SMEM), anywhere]
    if fused:
        second = (tiles_y, tiles_x, cells_x, levels_z)
        scratch += [
            pltpu.VMEM((cells_x * cells_y, levels_z), jnp.float32),
            pltpu.VMEM((parts, cells_x, levels_z), jnp.float32),
            dma((parts * tiles_y,)), dma,
        ]
    else:
        second = (cells_x, cells_y, levels_z)
    field_out, other = pl.pallas_call(
        functools.partial(step_kernel, sizes, fused),
        out_shape=(
            jax.ShapeDtypeStruct(velocity.shape, jnp.float32),
            jax.ShapeDtypeStruct(second, jnp.float32),
        ),
        in_specs=in_specs,
        out_specs=(anywhere, vmem),
        scratch_shapes=scratch,
        compiler_params=pltpu.CompilerParams(
            collective_id=0, has_side_effects=True, vmem_limit_bytes=60 * 1024 * 1024
        ),
        name="farm_step",
    )(*args)
    if fused:
        along, across = tables(tiles_y, total_x, total_y, levels_z // (2 * waves))
        result = (2, depth, waves, total_y)
        return pl.pallas_call(
            functools.partial(transform_kernel, sizes),
            out_shape=(
                jax.ShapeDtypeStruct(velocity.shape, jnp.float32),
                jax.ShapeDtypeStruct(result, jnp.float32),
            ),
            in_specs=[anywhere] * 4,
            out_specs=(anywhere, anywhere),
            scratch_shapes=[
                pltpu.VMEM(result, jnp.float32),
                pltpu.VMEM((tiles_y * levels_z, levels_z), jnp.float32),
                pltpu.VMEM(second, jnp.float32),
                pltpu.VMEM(along.shape[1:], jnp.float32),
                pltpu.VMEM(across.shape, jnp.float32),
                pltpu.VMEM(velocity.shape, jnp.float32),
                dma((6,)),
            ],
            compiler_params=pltpu.CompilerParams(vmem_limit_bytes=60 * 1024 * 1024),
            name="transform",
        )(other, jnp.asarray(along), jnp.asarray(across), field_out)
    return field_out, spectrum_of(other)


def spectrum_of(divergence):
    cells_x, cells_y, levels_z = divergence.shape
    tiles_x = lax.axis_size("gx")
    total_x, total_y = cells_x * tiles_x, cells_y * lax.axis_size("gy")
    is_farm = lax.axis_index("dom") == 1
    levels_out = levels_z // (2 * tiles_x)
    tile_block = divergence.reshape(cells_x, cells_y, 2, tiles_x, levels_out)
    highest = lax.Precision.HIGHEST
    cos_table_x, sin_table_x = dft_tables(total_x)
    cos_table_y, sin_table_y = dft_tables(total_y)
    shard_piece = lax.all_to_all(tile_block, "gx", split_axis=3, concat_axis=0, tiled=True)
    real_part = jnp.einsum("xyhgc,xk->yhck", shard_piece, cos_table_x, precision=highest)
    imag_part = -jnp.einsum("xyhgc,xk->yhck", shard_piece, sin_table_x, precision=highest)
    real_part, imag_part = (real_part, imag_part)
    real_in = lax.all_to_all(real_part, "gy", split_axis=3, concat_axis=0, tiled=True)
    imag_in = lax.all_to_all(imag_part, "gy", split_axis=3, concat_axis=0, tiled=True)
    real_out = jnp.einsum("yhck,yj->hckj", real_in, cos_table_y, precision=highest) + jnp.einsum(
        "yhck,yj->hckj", imag_in, sin_table_y, precision=highest
    )
    imag_out = jnp.einsum("yhck,yj->hckj", imag_in, cos_table_y, precision=highest) - jnp.einsum(
        "yhck,yj->hckj", real_in, sin_table_y, precision=highest
    )
    packed = jnp.stack([real_out, imag_out])
    received = partner_half(packed[:, 0])
    spectrum = jnp.where(is_farm, packed[:, 1], received)
    return spectrum


def solution(mesh):
    in_specs = (P("dom", None, "gx", "gy", None), P())
    out_specs = (P("dom", None, "gx", "gy", None), P(None, ("dom", "gx"), "gy", None))
    return jax.shard_map(
        functools.partial(on_device, mesh.shape["gx"], mesh.shape["gy"]),
        mesh=mesh, in_specs=in_specs, out_specs=out_specs, check_vma=False,
    )
```

```python
import functools
import math

import jax
import jax.numpy as jnp
import numpy as np
from jax import lax
from jax.experimental import pallas as pl
from jax.experimental.pallas import tpu as pltpu
from jax.sharding import PartitionSpec as P

time_step = 0.1
fringe_rate = 1.0
smag_coef = 0.03
base_visc = 0.02
strain_floor = 0.25
MESH = pl.DeviceIdType.MESH
WIDE = 4
BASE = 8


def from_behind(shard, axis, by):
    peers = lax.axis_size(axis)
    pairs = [(i, i + by) for i in range(peers) if 0 <= i + by < peers]
    return lax.ppermute(shard, axis, pairs)


def partner_half(values):
    return from_behind(values, "dom", -1)


def dft_tables(length):
    positions = jnp.arange(length, dtype=jnp.int32)
    phase = (positions[:, None] * positions[None, :] % length).astype(jnp.float32) * (
        2.0 * math.pi / length
    )
    factor = 1.0 / math.sqrt(length)
    return (jnp.cos(phase) * factor, jnp.sin(phase) * factor)


def step_kernel(sizes, fused, *refs):
    tiles_x, tiles_y, cells_x, cells_y, levels_z, fringe_len = sizes
    if fused:
        (fs_ref, u_hbm, v_hbm, got, *scratch) = refs
    else:
        (fs_ref, u_hbm, v_hbm, div_ref, *scratch) = refs
    (U, I, S1, S2, S3, edge, near, near_in, tips, diag, diag_in, ramp) = scratch[:12]
    (load_sem, send_sem, recv_sem, in_send, in_recv, out_sem) = scratch[12:18]
    if fused:
        rows, block, blk_send, blk_recv = scratch[18:]
    dom, gx, gy = (lax.axis_index(name) for name in ("dom", "gx", "gy"))
    count = 2 * tiles_x * tiles_y
    me = (dom * tiles_x + gx) * tiles_y + gy
    total_x = cells_x * tiles_x
    hi = WIDE + cells_x
    inner = pl.ds(BASE, cells_y)

    def at(index):
        return (
            index // (tiles_x * tiles_y),
            lax.rem(index // tiles_y, tiles_x),
            lax.rem(index, tiles_y),
        )

    def beside(domain, dx, dy):
        return (
            domain,
            lax.rem(gx + dx + tiles_x, tiles_x),
            lax.rem(gy + dy + tiles_y, tiles_y),
        )

    around = [(1, 0), (-1, 0), (0, 1), (0, -1), (1, 1), (1, -1), (-1, 1), (-1, -1)]
    barrier = pltpu.get_barrier_semaphore()
    if fused:
        @pl.loop(1, count)
        def _(i):
            pl.semaphore_signal(
                barrier, inc=1, device_id=at(lax.rem(me + i, count)), device_id_type=MESH
            )
    else:
        for dx, dy in around:
            for domain in range(2):
                pl.semaphore_signal(
                    barrier, inc=1, device_id=beside(domain, dx, dy), device_id_type=MESH
                )
        pl.semaphore_signal(barrier, inc=1, device_id=beside(1 - dom, 0, 0), device_id_type=MESH)

    load = pltpu.make_async_copy(u_hbm.at[0], U.at[:, pl.ds(WIDE, cells_x), inner, :], load_sem)
    load.start()

    cell = lax.broadcasted_iota(jnp.int32, ramp.shape, 0) + (gx * cells_x - WIDE)
    offset = cell - fs_ref[0]
    for _ in range(2):
        offset = jnp.where(offset < 0, offset + total_x, offset)
    offset = jnp.where(offset >= total_x, offset - total_x, offset)
    sine = jnp.sin((offset.astype(jnp.float32) + 0.5) * (math.pi / fringe_len))
    farm = dom.astype(jnp.float32)
    ramp[...] = jnp.where(offset < fringe_len, fringe_rate * sine * sine, 0.0) * farm

    @pl.when(dom == 0)
    def _():
        I[...] = jnp.zeros_like(I)

    load.wait()
    for side in range(2):
        start = BASE if side == 0 else BASE + cells_y - WIDE
        for c in range(3):
            for j in range(WIDE):
                edge[side, c, j] = U[c, WIDE:hi, start + j, :]
        tips[0, side] = U[:, hi - WIDE : hi, start : start + WIDE, :]
        tips[1, side] = U[:, WIDE : 2 * WIDE, start : start + WIDE, :]
    pl.semaphore_wait(barrier, count - 1 if fused else 17)

    def margins(domain, field, strips, corners, sends, recvs, width):
        low, high = pl.ds(WIDE - width, width), pl.ds(hi, width)
        less = width - 1
        pieces = []
        for dx, dy in around:
            mine = pl.ds(hi - width, width) if dx > 0 else pl.ds(WIDE, width)
            side = 1 if dy > 0 else 0
            span = pl.ds(WIDE - width if dy > 0 else 0, width)
            if dy == 0:
                pieces.append((U.at[:, mine, inner, :], field.at[:, low if dx > 0 else high, inner, :]))
            elif dx == 0:
                pieces.append((edge.at[side, :, span], strips.at[1 - side, :, span]))
            else:
                part = pl.ds(WIDE - less if dx > 0 else 0, less)
                pieces.append((
                    tips.at[0 if dx > 0 else 1, side, :, part],
                    corners.at[0 if dx > 0 else 1, 1 - side, :, part],
                ))
        return [
            pltpu.make_async_remote_copy(
                src_ref=source, dst_ref=target, send_sem=sends.at[i], recv_sem=recvs.at[i],
                device_id=beside(domain, *around[i]), device_id_type=MESH,
            )
            for i, (source, target) in enumerate(pieces)
        ]

    def onward(width):
        less = width - 1
        pairs = []
        for dx, dy in around:
            side = 0 if dy > 0 else 1
            span = pl.ds(WIDE - width if dy > 0 else 0, width)
            slab = pl.ds(WIDE - width if dx > 0 else hi, width)
            part = (0 if dx > 0 else 1, side, slice(None), pl.ds(WIDE - less if dx > 0 else 0, less))
            if dy == 0:
                pairs.append((U.at[:, slab, inner, :], I.at[:, slab, inner, :]))
            elif dx == 0:
                pairs.append((near.at[side, :, span], near_in.at[side, :, span]))
            else:
                pairs.append((diag.at[part], diag_in.at[part]))
        return [
            pltpu.make_async_remote_copy(
                src_ref=source, dst_ref=target, send_sem=in_send.at[i], recv_sem=in_recv.at[i],
                device_id=(1 - dom, gx, gy), device_id_type=MESH,
            )
            for i, (source, target) in enumerate(pairs)
        ]

    def place(field, strips, corners):
        for side in range(2):
            start = BASE - WIDE if side == 0 else BASE + cells_y
            span = pl.ds(start, WIDE)
            for c in range(3):
                for j in range(WIDE):
                    field[c, WIDE:hi, start + j, :] = strips[side, c, j]
            field[:, 0:WIDE, span, :] = corners[0, side]
            field[:, hi : hi + WIDE, span, :] = corners[1, side]

    to_pre = margins(0, U, near, diag, send_sem, recv_sem, WIDE - 1)
    to_farm = margins(1, U, near, diag, send_sem, recv_sem, WIDE)
    inflow = onward(WIDE - 1)
    block_in = pltpu.make_async_remote_copy(
        src_ref=U.at[:, pl.ds(WIDE, cells_x), inner, :],
        dst_ref=I.at[:, pl.ds(WIDE, cells_x), inner, :],
        send_sem=in_send.at[8], recv_sem=in_recv.at[8],
        device_id=(1 - dom, gx, gy), device_id_type=MESH,
    )
    order = [4, 5, 6, 7, 2, 3, 0, 1]

    @pl.when(dom == 0)
    def _():
        for i in order:
            to_pre[i].start()
        block_in.start()
        for i in order:
            to_pre[i].wait_recv()
            inflow[i].start()
        place(U, near, diag)

    @pl.when(dom == 1)
    def _():
        for i in order:
            to_farm[i].start()
        for copy in to_farm:
            copy.wait_recv()
        place(U, near, diag)

    lane = lax.broadcasted_iota(jnp.int32, (8, levels_z), 1)
    first, last = lane == 0, lane == levels_z - 1

    def rate(field, x, row, pulled=True):
        centre = [field[c, x, pl.ds(row, 8), :] for c in range(3)]
        grads, laps = [[], [], []], []
        for c in range(3):
            xp, xm = field[c, x + 1, pl.ds(row, 8), :], field[c, x - 1, pl.ds(row, 8), :]
            yp, ym = field[c, x, pl.ds(row + 1, 8), :], field[c, x, pl.ds(row - 1, 8), :]
            zp = jnp.where(last, 0.0, pltpu.roll(centre[c], levels_z - 1, 1))
            zm = jnp.where(first, 0.0, pltpu.roll(centre[c], 1, 1))
            grads[0].append(xp - xm)
            grads[1].append(yp - ym)
            grads[2].append(zp - zm)
            laps.append((xp + xm) + (yp + ym) + (zp + zm) - 6.0 * centre[c])
        (axx, axy, axz), (ayx, ayy, ayz), (azx, azy, azz) = grads
        shear = (axy + ayx, axz + azx, ayz + azy)
        diagonal = axx * axx + ayy * ayy + azz * azz
        sheared = shear[0] * shear[0] + shear[1] * shear[1] + shear[2] * shear[2]
        under = 0.5 * diagonal + (0.25 * sheared + strain_floor)
        eddy = base_visc + smag_coef * (under * lax.rsqrt(under))
        pull = jnp.broadcast_to(ramp[pl.ds(x, 1), :], (8, levels_z))
        rates = []
        for c in range(3):
            carried = centre[0] * grads[0][c] + centre[1] * grads[1][c] + centre[2] * grads[2][c]
            free = eddy * laps[c] - 0.5 * carried
            if pulled:
                free = free + pull * (I[c, x, pl.ds(row, 8), :] - centre[c])
            rates.append(free)
        return centre, rates

    def stage(field, result, margin, finish, pulled=True):
        starts = (BASE - margin, BASE + cells_y + margin - 8)

        @pl.loop(WIDE - margin, hi + margin, unroll=cells_x + 2 * margin)
        def _(x):
            for row in starts:
                centre, rates = rate(field, x, row, pulled)
                for c in range(3):
                    result[c, x, pl.ds(row, 8), :] = finish(
                        U[c, x, pl.ds(row, 8), :], centre[c] + time_step * rates[c]
                    )

    stage(U, S1, 3, lambda start, moved: moved, pulled=False)

    @pl.when(dom == 1)
    def _():
        for copy in inflow:
            copy.wait_recv()
        block_in.wait_recv()
        place(I, near_in, diag_in)

        @pl.loop(WIDE - 3, hi + 3, unroll=2)
        def _(x):
            pull = time_step * jnp.broadcast_to(ramp[pl.ds(x, 1), :], (8, levels_z))
            for row in (BASE - 3, BASE + 5):
                for c in range(3):
                    S1[c, x, pl.ds(row, 8), :] += pull * (
                        I[c, x, pl.ds(row, 8), :] - U[c, x, pl.ds(row, 8), :]
                    )

    stage(S1, S2, 2, lambda start, moved: 0.75 * start + 0.25 * moved)
    stage(S2, S3, 1, lambda start, moved: (1.0 / 3.0) * start + (2.0 / 3.0) * moved)

    out = pltpu.make_async_copy(S3.at[:, pl.ds(WIDE, cells_x), inner, :], v_hbm.at[0], out_sem)
    out.start()

    def divergence(x):
        w = S3[2, x, inner, :]
        up = jnp.where(last, 0.0, pltpu.roll(w, levels_z - 1, 1))
        down = jnp.where(first, 0.0, pltpu.roll(w, 1, 1))
        along = 0.5 * (S3[0, x + 1, inner, :] - S3[0, x - 1, inner, :])
        across = 0.5 * (S3[1, x, pl.ds(BASE + 1, 8), :] - S3[1, x, pl.ds(BASE - 1, 8), :])
        return along + across + 0.5 * (up - down)

    if not fused:
        for x in range(cells_x):
            div_ref[x] = divergence(x + WIDE)
    else:
        parts = 2 * tiles_x
        depth = levels_z // parts
        group = lax.broadcasted_iota(jnp.int32, (cells_x, levels_z), 1) // depth

        def block_copy(i):
            target = lax.rem(me + i, count)
            return pltpu.make_async_remote_copy(
                src_ref=block.at[target // tiles_y], dst_ref=got.at[gy, gx],
                send_sem=blk_send.at[i], recv_sem=blk_recv,
                device_id=at(target), device_id_type=MESH,
            )

        @pl.when(dom == 1)
        def _():
            for x in range(cells_x):
                rows[x * cells_y : (x + 1) * cells_y, :] = divergence(x + WIDE)
            pieces = [None] * parts
            for y in range(cells_y):
                line = rows[pl.ds(y, cells_x, stride=cells_y), :]
                for p in range(parts):
                    by = ((y - p) * depth) % levels_z
                    moved = pltpu.roll(line, by, 1) if by else line
                    pieces[p] = moved if y == 0 else jnp.where(group == y, moved, pieces[p])
            for p in range(parts):
                block[p] = pieces[p]
            for i in range(1, count):
                block_copy(i).start()
            pltpu.make_async_copy(block.at[me // tiles_y], got.at[gy, gx], blk_recv).start()

        pltpu.make_async_copy(got, got, blk_recv).wait()

        @pl.when(dom == 1)
        def _():
            for i in range(1, count):
                block_copy(i).wait_send()

    @pl.when(dom == 1)
    def _():
        for copy in to_farm:
            copy.wait_send()

    @pl.when(dom == 0)
    def _():
        for copy in to_pre + inflow:
            copy.wait_send()
        block_in.wait_send()

    out.wait()


def transform_kernel(
    sizes, got_hbm, tx_hbm, ty_hbm, v_from, v_hbm, spec_hbm, spec_ref, turned, got, tx, ty, v_ref, sems
):
    tiles_x, tiles_y, cells_x, cells_y, levels_z, _ = sizes
    gy = lax.axis_index("gy")
    total_x = cells_x * tiles_x
    depth = levels_z // (2 * tiles_x)
    loads = [
        pltpu.make_async_copy(source, target, sems.at[i + 2])
        for i, (source, target) in enumerate(
            [(got_hbm, got), (tx_hbm.at[gy], tx), (ty_hbm, ty), (v_from, v_ref)]
        )
    ]
    for load in loads:
        load.start()
    save = pltpu.make_async_copy(v_ref, v_hbm, sems.at[0])
    for load in loads[:3]:
        load.wait()
    highest = lax.Precision.HIGHEST
    for g in range(tiles_y):
        lines = got[g].reshape(total_x, levels_z)
        partly = jnp.dot(tx[...], lines, precision=highest, preferred_element_type=jnp.float32)
        turned[g * levels_z : (g + 1) * levels_z, :] = partly.T
    total_y = cells_y * tiles_y
    waves = total_x // tiles_y
    wide = 2 * waves
    each = levels_z // wide
    chunk = lax.broadcasted_iota(jnp.int32, (total_y, levels_z), 1) // wide
    loads[3].wait()
    save.start()
    for q in range(depth // each):
        packed = None
        for j in range(each):
            level = turned[pl.ds(q * each + j, total_y, stride=depth), :]
            packed = level if j == 0 else jnp.where(chunk == j, level, packed)
        both = jnp.dot(packed.T, ty[...], precision=highest, preferred_element_type=jnp.float32)
        for j in range(each):
            real = both[j * wide : j * wide + waves]
            imag = both[j * wide + waves : (j + 1) * wide]
            whole = real + pltpu.roll(imag, 2 * total_y, 1)
            spec_ref[0, q * each + j] = whole[:, :total_y]
            spec_ref[1, q * each + j] = whole[:, total_y : 2 * total_y]
    store = pltpu.make_async_copy(spec_ref, spec_hbm, sems.at[1])
    store.start()
    store.wait()
    save.wait()


def tables(tiles_y, total_x, total_y, each):
    waves = total_x // tiles_y
    turn = 2.0 * np.pi / total_x * (np.outer(np.arange(total_x), np.arange(total_x)) % total_x)
    cosine, sine = np.cos(turn) / np.sqrt(total_x), -np.sin(turn) / np.sqrt(total_x)
    along = np.stack([cosine.reshape(tiles_y, waves, total_x), sine.reshape(tiles_y, waves, total_x)], 1)
    along = np.tile(along.reshape(tiles_y, 2 * waves, total_x), (1, each, 1))
    turn = 2.0 * np.pi / total_y * (np.outer(np.arange(total_y), np.arange(total_y)) % total_y)
    cosine, sine = np.cos(turn) / np.sqrt(total_y), np.sin(turn) / np.sqrt(total_y)
    across = np.concatenate([cosine, -sine, sine, cosine], 1)
    return along.astype(np.float32), across.astype(np.float32)


def on_device(tiles_x, tiles_y, velocity, fringe_start):
    _, _, cells_x, cells_y, levels_z = velocity.shape
    total_x, total_y = cells_x * tiles_x, cells_y * tiles_y
    fringe_len = min(8 * cells_x, total_x // 2)
    parts = 2 * tiles_x
    depth = levels_z // parts
    waves = total_x // tiles_y
    fused = cells_y * depth == levels_z and 4 * total_y == levels_z and 8 * waves == levels_z
    sizes = (tiles_x, tiles_y, cells_x, cells_y, levels_z, fringe_len)
    field = pltpu.VMEM((3, cells_x + 2 * WIDE, cells_y + 2 * BASE, levels_z), jnp.float32)
    strips = pltpu.VMEM((2, 3, WIDE, cells_x, levels_z), jnp.float32)
    corners = pltpu.VMEM((2, 2, 3, WIDE, WIDE, levels_z), jnp.float32)
    dma = pltpu.SemaphoreType.DMA
    scratch = [field] * 5 + [strips] * 3 + [corners] * 3
    scratch += [pltpu.VMEM((cells_x + 2 * WIDE, levels_z), jnp.float32)]
    scratch += [dma, dma((8,)), dma((8,)), dma((9,)), dma((9,)), dma]
    anywhere, vmem = pl.BlockSpec(memory_space=pltpu.HBM), pl.BlockSpec(memory_space=pltpu.VMEM)
    args = [fringe_start, velocity]
    in_specs = [pl.BlockSpec(memory_space=pltpu.SMEM), anywhere]
    if fused:
        second = (tiles_y, tiles_x, cells_x, levels_z)
        scratch += [
            pltpu.VMEM((cells_x * cells_y, levels_z), jnp.float32),
            pltpu.VMEM((parts, cells_x, levels_z), jnp.float32),
            dma((parts * tiles_y,)), dma,
        ]
    else:
        second = (cells_x, cells_y, levels_z)
    field_out, other = pl.pallas_call(
        functools.partial(step_kernel, sizes, fused),
        out_shape=(
            jax.ShapeDtypeStruct(velocity.shape, jnp.float32),
            jax.ShapeDtypeStruct(second, jnp.float32),
        ),
        in_specs=in_specs,
        out_specs=(anywhere, vmem),
        scratch_shapes=scratch,
        compiler_params=pltpu.CompilerParams(
            collective_id=0, has_side_effects=True, vmem_limit_bytes=60 * 1024 * 1024
        ),
        name="farm_step",
    )(*args)
    if fused:
        along, across = tables(tiles_y, total_x, total_y, levels_z // (2 * waves))
        result = (2, depth, waves, total_y)
        return pl.pallas_call(
            functools.partial(transform_kernel, sizes),
            out_shape=(
                jax.ShapeDtypeStruct(velocity.shape, jnp.float32),
                jax.ShapeDtypeStruct(result, jnp.float32),
            ),
            in_specs=[anywhere] * 4,
            out_specs=(anywhere, anywhere),
            scratch_shapes=[
                pltpu.VMEM(result, jnp.float32),
                pltpu.VMEM((tiles_y * levels_z, levels_z), jnp.float32),
                pltpu.VMEM(second, jnp.float32),
                pltpu.VMEM(along.shape[1:], jnp.float32),
                pltpu.VMEM(across.shape, jnp.float32),
                pltpu.VMEM(velocity.shape, jnp.float32),
                dma((6,)),
            ],
            compiler_params=pltpu.CompilerParams(vmem_limit_bytes=60 * 1024 * 1024),
            name="transform",
        )(other, jnp.asarray(along), jnp.asarray(across), field_out)
    return field_out, spectrum_of(other)


def spectrum_of(divergence):
    cells_x, cells_y, levels_z = divergence.shape
    tiles_x = lax.axis_size("gx")
    total_x, total_y = cells_x * tiles_x, cells_y * lax.axis_size("gy")
    is_farm = lax.axis_index("dom") == 1
    levels_out = levels_z // (2 * tiles_x)
    tile_block = divergence.reshape(cells_x, cells_y, 2, tiles_x, levels_out)
    highest = lax.Precision.HIGHEST
    cos_table_x, sin_table_x = dft_tables(total_x)
    cos_table_y, sin_table_y = dft_tables(total_y)
    shard_piece = lax.all_to_all(tile_block, "gx", split_axis=3, concat_axis=0, tiled=True)
    real_part = jnp.einsum("xyhgc,xk->yhck", shard_piece, cos_table_x, precision=highest)
    imag_part = -jnp.einsum("xyhgc,xk->yhck", shard_piece, sin_table_x, precision=highest)
    real_part, imag_part = (real_part, imag_part)
    real_in = lax.all_to_all(real_part, "gy", split_axis=3, concat_axis=0, tiled=True)
    imag_in = lax.all_to_all(imag_part, "gy", split_axis=3, concat_axis=0, tiled=True)
    real_out = jnp.einsum("yhck,yj->hckj", real_in, cos_table_y, precision=highest) + jnp.einsum(
        "yhck,yj->hckj", imag_in, sin_table_y, precision=highest
    )
    imag_out = jnp.einsum("yhck,yj->hckj", imag_in, cos_table_y, precision=highest) - jnp.einsum(
        "yhck,yj->hckj", real_in, sin_table_y, precision=highest
    )
    packed = jnp.stack([real_out, imag_out])
    received = partner_half(packed[:, 0])
    spectrum = jnp.where(is_farm, packed[:, 1], received)
    return spectrum


def solution(mesh):
    in_specs = (P("dom", None, "gx", "gy", None), P())
    out_specs = (P("dom", None, "gx", "gy", None), P(None, ("dom", "gx"), "gy", None))
    return jax.shard_map(
        functools.partial(on_device, mesh.shape["gx"], mesh.shape["gy"]),
        mesh=mesh, in_specs=in_specs, out_specs=out_specs, check_vma=False,
    )
```
